128 devices in a mesh: fsdp: 8 (over y, x_hi), seq: 16 (over x_lo, z, core).
Axes of the slice: x: 4 (x_hi: 2, x_lo: 2; x = x_hi * 2 + x_lo), y: 4, z: 4, core: 2. Of those that a mesh axis runs over, the one named last changes fastest.
Arguments:
- hidden_in: bfloat16 [8, 4096, 4096], P('fsdp', 'seq'), may hold values from -6 to 6
- queries: bfloat16 [8, 4096, 2048], P('fsdp', 'seq'), may hold values from -8 to 8
- keys: bfloat16 [8, 4096, 2048], P('fsdp', 'seq'), may hold values from -8 to 8
- values: bfloat16 [8, 4096, 2048], P('fsdp', 'seq'), may hold values from -6 to 6
- block_start: int32 [32], P('seq'), may hold values from 0 to 3968, as said below
- out_weight: bfloat16 [2048, 4096], P('fsdp'), may hold values from -0.125 to 0.125
Outputs:
- mixed: bfloat16 [8, 4096, 4096], P('fsdp', 'seq')
The draws below stay inside these ranges and needn't reach their ends.
Inputs may be any that keep to these rules, and one draw needn't show every extreme that they name: block_start is 128 times a permutation of 0 to 31.
All inputs are finite; a program needn't handle non-finite values.
Results may differ from the reference program's by a relative error of at most 0.006.
Values may be sent and summed in bfloat16 or wider, within the bound.
No kernel may reach another device: no remote copies, remote signals or barrier semaphores. Data moves between devices by JAX's collectives and lax.ppermute only.
A program may use at most 192 MiB of HBM per device.

```python
import math
import jax
import jax.numpy as jnp
from jax import lax

D = 4096
HEADS = 16
HEAD_DIM = 128
HALF = 128
LEN = 4096
BLOCKS = 32
SEQS = 8


def draw_queries(key, part):
    key = jax.random.fold_in(key, 7)
    shape = (SEQS, LEN, HEADS * HEAD_DIM)
    base = jnp.clip(jax.random.normal(key, shape, jnp.float32), -4.0, 4.0)
    return base.astype(jnp.bfloat16)


def draw_keys(key, part):
    key = jax.random.fold_in(key, 13)
    shape = (SEQS, LEN, HEADS * HEAD_DIM)
    base = jnp.clip(jax.random.normal(key, shape, jnp.float32), -4.0, 4.0)
    return base.astype(jnp.bfloat16)


def draw_block_start(key, part):
    key = jax.random.fold_in(key, 3)
    return (jax.random.permutation(key, BLOCKS) * HALF).astype(jnp.int32)


def levels(own_key, dims, shards, least, top_value):
    factor_of, own = 1.0, jax.random.fold_in(own_key, 6)
    for dim, parts in shards:
        draws = jnp.exp(jax.random.uniform(jax.random.fold_in(own, dim), (parts,), jnp.float32, least / len(shards), top_value / len(shards)))
        factor_of = factor_of * jnp.repeat(draws, dims[dim] // parts).reshape([-1 if axis == dim else 1 for axis in range(len(dims))])
    return factor_of


def noise(own_key, dims, scale, bound, pieces=(), held_as=jnp.bfloat16):
    array = scale * jax.random.normal(own_key, dims, jnp.float32)
    if pieces:
        array = array * levels(own_key, dims, pieces, -0.22, 0.18)
    return jnp.clip(array, -bound, bound).astype(held_as)


def setup_inputs(seed: int = 0) -> dict:
    seeds = jax.random.split(jax.random.key(seed), 7)
    return {
        "hidden_in": noise(seeds[0], (SEQS, LEN, D), 1.0, 6.0, ((0, 8), (1, 16))),
        "queries": draw_queries(jax.random.fold_in(seeds[6], 71), 0),
        "keys": draw_keys(jax.random.fold_in(seeds[6], 71), 0),
        "values": noise(seeds[3], (SEQS, LEN, HEADS * HEAD_DIM), 1.0, 6.0, ((0, 8), (1, 16))),
        "block_start": draw_block_start(jax.random.fold_in(seeds[6], 71), 0),
        "out_weight": noise(seeds[5], (HEADS * HEAD_DIM, D), (HEADS * HEAD_DIM) ** -0.5, 0.125, ((0, 8),)),
    }


def rotate(source, positions):
    rows_here = source.shape[0]
    width = source.shape[1]
    half_dim = HEAD_DIM // 2
    spread = source.astype(jnp.float32).reshape(rows_here, width // HEAD_DIM, HEAD_DIM)
    frequency = 10000.0 ** (-jnp.arange(half_dim, dtype=jnp.float32) / half_dim)
    angles = positions.astype(jnp.float32)[:, None] * frequency[None, :]
    cosine = jnp.cos(angles)[:, None, :]
    sine = jnp.sin(angles)[:, None, :]
    first_half = spread[:, :, :half_dim]
    second_half = spread[:, :, half_dim:]
    turned = jnp.concatenate([first_half * cosine - second_half * sine, second_half * cosine + first_half * sine], axis=-1)
    return turned.reshape(rows_here, width).astype(jnp.bfloat16)

def reference(hidden_in, queries, keys, values, block_start, out_weight):
    rows_all = jnp.arange(LEN, dtype=jnp.int32)
    positions = block_start[rows_all // HALF] + rows_all % HALF
    allowed = positions[None, :] <= positions[:, None]
    scale = 1.0 / math.sqrt(HEAD_DIM)

    def one_sequence(items):
        hidden_row, query_row, key_row, value_row = items
        q_rot = rotate(query_row, positions).reshape(LEN, HEADS, HEAD_DIM).transpose(1, 0, 2)
        k_rot = rotate(key_row, positions).reshape(LEN, HEADS, HEAD_DIM).transpose(1, 0, 2)
        value_heads = value_row.reshape(LEN, HEADS, HEAD_DIM).transpose(1, 0, 2)

        def one_head(head_items):
            query_head, key_head, value_head = head_items
            scores = jnp.dot(query_head, key_head.T, preferred_element_type=jnp.float32) * scale
            scores = jnp.where(allowed, scores, -jnp.inf)
            highest = lax.optimization_barrier(jnp.max(scores, axis=1, keepdims=True))
            weights = jnp.where(allowed, jnp.exp(scores - highest), 0.0)
            denominator = lax.optimization_barrier(jnp.sum(weights, axis=1))
            probs = weights.astype(jnp.bfloat16)
            summed = jnp.dot(probs, value_head, preferred_element_type=jnp.float32)
            return (summed / denominator[:, None]).astype(jnp.bfloat16)
        heads_out = lax.map(one_head, (q_rot, k_rot, value_heads))
        attended = heads_out.transpose(1, 0, 2).reshape(LEN, HEADS * HEAD_DIM)
        mixed = hidden_row.astype(jnp.float32) + jnp.dot(attended, out_weight, preferred_element_type=jnp.float32)
        return mixed.astype(jnp.bfloat16)
    return lax.map(one_sequence, (hidden_in, queries, keys, values))
```

```python
import functools
import itertools
import math

import jax
import jax.numpy as jnp
import numpy as np
from jax import lax
from jax.experimental import pallas as pl
from jax.experimental.pallas import tpu as pltpu
from jax.sharding import Mesh
from jax.sharding import PartitionSpec as P

HEADS = 16
HEAD_DIM = 128
LEN = 4096
HALF = 128
WIDTH = HEADS * HEAD_DIM
D = 4096
ROWS = 3 * HALF + 16
AXES = ("y", "xh", "xl", "z", "c")
SIZES = (4, 2, 2, 4, 2)
FSDP = ("y", "xh")
SEQ = ("xl", "z", "c")
VMEM = 56 * 2**20


def tables():
    frequency = 10000.0 ** (-np.arange(HEAD_DIM // 2) / (HEAD_DIM // 2))
    angles = np.arange(LEN)[:, None] * frequency[None, :]
    cosine, sine = np.cos(angles), np.sin(angles)
    return (
        np.concatenate([cosine, cosine], axis=1).astype(np.float32),
        np.concatenate([-sine, sine], axis=1).astype(np.float32),
    )


def send(array, move):
    places = list(itertools.product(*map(range, SIZES)))
    index = {place: i for i, place in enumerate(places)}
    return lax.ppermute(array, AXES, [(index[p], index[move(*p)]) for p in places])


def y_up(y, xh, xl, z, c):
    return ((y + 1) % 4, xh, xl, z, c)


def y_down(y, xh, xl, z, c):
    return ((y + 3) % 4, xh, xl, z, c)


def x_over(y, xh, xl, z, c):
    return (y, 1 - xh, 1 - xl, z, c)


def core_over(y, xh, xl, z, c):
    return (y, xh, xl, z, 1 - c)


def pack_kernel(starts, q_ref, k_ref, v_ref, cos_ref, sin_ref, out_ref):
    cosine, sine = cos_ref[...], sin_ref[...]
    factor = math.log2(math.e) / math.sqrt(HEAD_DIM)

    def turn(block, cosine, sine):
        block = block.astype(jnp.float32)
        turned = block * cosine + pltpu.roll(block, HEAD_DIM // 2, 1) * sine
        return turned.astype(jnp.bfloat16)

    for h in range(HEADS):
        lanes = slice(h * HEAD_DIM, (h + 1) * HEAD_DIM)
        out_ref[h, 0, 0:HALF] = turn(q_ref[:, lanes], cosine * factor, sine * factor)
        out_ref[h, 0, HALF : 2 * HALF] = turn(k_ref[:, lanes], cosine, sine)
        out_ref[h, 0, 2 * HALF : 3 * HALF] = v_ref[:, lanes]
    block = (starts[pl.program_id(0)] // HALF).astype(jnp.float32)
    out_ref[:, 0, 3 * HALF :] = jnp.full((HEADS, 16, HEAD_DIM), block, jnp.float32).astype(
        jnp.bfloat16
    )


def pack(starts, queries, keys, values):
    cosine, sine = tables()
    rows = pl.BlockSpec((HALF, WIDTH), lambda b, s: (b, 0))
    table = pl.BlockSpec((HALF, HEAD_DIM), lambda b, s: (s[b] // HALF, 0))
    return pl.pallas_call(
        pack_kernel,
        grid_spec=pltpu.PrefetchScalarGridSpec(
            num_scalar_prefetch=1,
            grid=(2,),
            in_specs=[rows, rows, rows, table, table],
            out_specs=pl.BlockSpec((HEADS, 1, ROWS, HEAD_DIM), lambda b, s: (0, b, 0, 0)),
        ),
        out_shape=jax.ShapeDtypeStruct((HEADS, 2, ROWS, HEAD_DIM), jnp.bfloat16),
        compiler_params=pltpu.CompilerParams(vmem_limit_bytes=VMEM),
        name="pack",
    )(starts, queries, keys, values, jnp.asarray(cosine), jnp.asarray(sine))


def attention_kernel(pos_ref, x_ref, o_ref, qs, kt, vs, scores, acc, high, *, tq):
    tiles = LEN // tq
    vs[:, HEAD_DIM:] = jnp.ones((LEN, HEAD_DIM), jnp.bfloat16)

    def place(t, carry):
        at = pl.ds(pl.multiple_of(pos_ref[t] * HALF, HALF), HALF)
        s, b = t // 2, t % 2
        qs[at, :] = x_ref[s, b, 0:HALF, :]
        kt[:, at] = x_ref[s, b, HALF : 2 * HALF, :].T
        vs[at, :HEAD_DIM] = x_ref[s, b, 2 * HALF : 3 * HALF, :]
        return carry

    lax.fori_loop(0, 2 * HEADS, place, 0, unroll=4)

    def span(i):
        return pl.ds(pl.multiple_of(i * tq, tq), tq)

    def product(i, j):
        return jnp.dot(qs[span(i), :], kt[:, span(j)], preferred_element_type=jnp.float32)

    def lane_max(s):
        m = s[:, :128]
        for c in range(1, tq // 128):
            m = jnp.maximum(m, s[:, c * 128 : (c + 1) * 128])
        return m

    row = lax.broadcasted_iota(jnp.int32, (tq, tq), 0)
    col = lax.broadcasted_iota(jnp.int32, (tq, tq), 1)

    def diagonal(i, slot):
        s = jnp.where(col <= row, product(i, i), -1e30)
        scores[slot, :, span(i)] = s
        return lane_max(s)

    high[...] = diagonal(0, 0)

    def tile(i, carry):
        now = lax.rem(i, 2)
        later = 1 - now
        m = jnp.broadcast_to(jnp.max(high[...], axis=1, keepdims=True), (tq, 128))
        high[...] = jnp.full((tq, 128), -1e30, jnp.float32)
        acc[...] = jnp.zeros((tq, 2 * HEAD_DIM), jnp.float32)
        following = jnp.minimum(i + 1, tiles - 1)

        def chunk(j, inner):
            s = scores[now, :, span(j)]
            p = jnp.concatenate(
                [
                    jnp.exp2(s[:, t * 128 : (t + 1) * 128] - m).astype(jnp.bfloat16)
                    for t in range(tq // 128)
                ],
                axis=1,
            )
            acc[...] += jnp.dot(p, vs[span(j), :], preferred_element_type=jnp.float32)
            ahead = product(following, j)
            scores[later, :, span(j)] = ahead
            high[...] = jnp.maximum(high[...], lane_max(ahead))
            return inner

        lax.fori_loop(0, i + 1, chunk, 0)

        @pl.when(i + 1 < tiles)
        def _():
            high[...] = jnp.maximum(high[...], diagonal(following, later))

        qs[span(i), :] = (acc[:, :HEAD_DIM] / acc[:, HEAD_DIM:]).astype(jnp.bfloat16)
        return carry

    lax.fori_loop(0, tiles, tile, 0)

    def unplace(t, carry):
        at = pl.ds(pl.multiple_of(pos_ref[t] * HALF, HALF), HALF)
        o_ref[t // 2, t % 2] = qs[at, :]
        return carry

    lax.fori_loop(0, 2 * HEADS, unplace, 0, unroll=4)


def attention(pos, packed, tq=512):
    return pl.pallas_call(
        functools.partial(attention_kernel, tq=tq),
        out_shape=jax.ShapeDtypeStruct((HEADS, 2, HALF, HEAD_DIM), jnp.bfloat16),
        in_specs=[
            pl.BlockSpec(memory_space=pltpu.SMEM),
            pl.BlockSpec(memory_space=pltpu.VMEM),
        ],
        out_specs=pl.BlockSpec(memory_space=pltpu.VMEM),
        scratch_shapes=[
            pltpu.VMEM((LEN, HEAD_DIM), jnp.bfloat16),
            pltpu.VMEM((HEAD_DIM, LEN), jnp.bfloat16),
            pltpu.VMEM((LEN, 2 * HEAD_DIM), jnp.bfloat16),
            pltpu.VMEM((2, tq, LEN), jnp.float32),
            pltpu.VMEM((tq, 2 * HEAD_DIM), jnp.float32),
            pltpu.VMEM((tq, 128), jnp.float32),
        ],
        compiler_params=pltpu.CompilerParams(vmem_limit_bytes=VMEM),
        cost_estimate=pl.CostEstimate(
            flops=2 * LEN * LEN * HEAD_DIM, bytes_accessed=4 * 2**20, transcendentals=LEN * LEN // 2
        ),
        name="attention",
    )(pos, packed)


PIECES = ((0, 0), (0, 1), (3, 0), (1, 0), (3, 1), (1, 1), (2, 0), (2, 1))
STEP = 512


def project_kernel(place, att_ref, hidden_ref, own_ref, *refs):
    mine, other, (out_ref, left) = refs[:8], refs[8:16], refs[16:]
    step = pl.program_id(0)

    @pl.when(step == 0)
    def _():
        for n in range(len(PIECES)):
            for t in range(2):
                head = att_ref[2 * place[1 + n] + t].reshape(2 * HALF, HEAD_DIM)
                left[:, (2 * n + t) * HEAD_DIM : (2 * n + t + 1) * HEAD_DIM] = head

    def total(blocks):
        rows = jnp.concatenate([own_ref[...]] + [b[...] for b in blocks], axis=0)
        summed = jnp.dot(left[...], rows, preferred_element_type=jnp.float32)
        out_ref[...] = (hidden_ref[...].astype(jnp.float32) + summed).astype(jnp.bfloat16)

    @pl.when(step < 4)
    def _():
        total(mine)

    @pl.when(step >= 4)
    def _():
        total(other)


def project(place, att, hidden, own, mine, other):
    def column(j, s):
        return (0, (s[0] * 4 + j) % 8)

    def spec(array, index):
        return pl.BlockSpec((array.shape[0], STEP), index)

    return pl.pallas_call(
        project_kernel,
        grid_spec=pltpu.PrefetchScalarGridSpec(
            num_scalar_prefetch=1,
            grid=(D // STEP,),
            in_specs=[
                pl.BlockSpec((HEADS, 2, HALF, HEAD_DIM), lambda j, s: (0, 0, 0, 0)),
                spec(hidden, column),
                spec(own, column),
                *[spec(a, lambda j, s: (0, jnp.minimum(j, 3))) for a in mine],
                *[spec(a, lambda j, s: (0, jnp.maximum(j - 4, 0))) for a in other],
            ],
            out_specs=pl.BlockSpec((2 * HALF, STEP), column),
            scratch_shapes=[pltpu.VMEM((2 * HALF, WIDTH), jnp.bfloat16)],
        ),
        out_shape=jax.ShapeDtypeStruct((2 * HALF, D), jnp.bfloat16),
        compiler_params=pltpu.CompilerParams(vmem_limit_bytes=VMEM),
        cost_estimate=pl.CostEstimate(
            flops=4 * HALF * WIDTH * D, bytes_accessed=20 * 2**20, transcendentals=0
        ),
        name="project",
    )(place, att, hidden, own, *mine, *other)


def shards(hidden_in, queries, keys, values, block_start, out_weight):
    y, xh, c = lax.axis_index("y"), lax.axis_index("xh"), lax.axis_index("c")
    packed = pack(block_start, queries[0], keys[0], values[0])
    packed = lax.all_to_all(packed, SEQ, 0, 0, tiled=True)

    half = lax.dynamic_slice(out_weight, (0, c * (D // 2)), (WIDTH // 8, D // 2))
    piece = {}
    piece[0, 1] = send(half, x_over)
    piece[3, 0] = send(half, y_up)
    piece[1, 0] = send(half, y_down)
    piece[3, 1] = send(piece[3, 0], x_over)
    piece[1, 1] = send(piece[0, 1], y_down)
    piece[2, 0] = send(piece[3, 0], y_up)
    top = send(piece[3, 1][:HALF], y_up)
    bottom = send(piece[1, 1][HALF:], y_down)
    mine = [piece[at] for at in PIECES[1:7]] + [top, bottom]
    other = [send(a, core_over) for a in mine]

    pos = packed[:, :, 3 * HALF, 0].reshape(2 * HEADS).astype(jnp.int32)
    attended = attention(pos, packed)
    attended = lax.all_to_all(attended, SEQ, 0, 0, tiled=True)

    owners = [((y + dy) % 4) * 2 + (xh + dx) % 2 for dy, dx in PIECES]
    place = jnp.stack([c, *owners]).astype(jnp.int32)
    return project(place, attended, hidden_in[0], out_weight, mine, other)[None]


def solution(mesh):
    fine = Mesh(mesh.devices.reshape(SIZES), AXES)
    return jax.shard_map(
        shards,
        mesh=fine,
        in_specs=(
            P(FSDP, SEQ, None),
            P(FSDP, SEQ, None),
            P(FSDP, SEQ, None),
            P(FSDP, SEQ, None),
            P(SEQ),
            P(FSDP, None),
        ),
        out_specs=P(FSDP, SEQ, None),
        check_vma=False,
    )
```

```python
import functools
import itertools
import math

import jax
import jax.numpy as jnp
import numpy as np
from jax import lax
from jax.experimental import pallas as pl
from jax.experimental.pallas import tpu as pltpu
from jax.sharding import Mesh
from jax.sharding import PartitionSpec as P

HEADS = 16
HEAD_DIM = 128
LEN = 4096
HALF = 128
WIDTH = HEADS * HEAD_DIM
D = 4096
ROWS = 3 * HALF + 16
AXES = ("y", "xh", "xl", "z", "c")
SIZES = (4, 2, 2, 4, 2)
FSDP = ("y", "xh")
SEQ = ("xl", "z", "c")
VMEM = 56 * 2**20


def tables():
    frequency = 10000.0 ** (-np.arange(HEAD_DIM // 2) / (HEAD_DIM // 2))
    angles = np.arange(LEN)[:, None] * frequency[None, :]
    cosine, sine = np.cos(angles), np.sin(angles)
    return (
        np.concatenate([cosine, cosine], axis=1).astype(np.float32),
        np.concatenate([-sine, sine], axis=1).astype(np.float32),
    )


def send(array, move):
    places = list(itertools.product(*map(range, SIZES)))
    index = {place: i for i, place in enumerate(places)}
    return lax.ppermute(array, AXES, [(index[p], index[move(*p)]) for p in places])


def y_up(y, xh, xl, z, c):
    return ((y + 1) % 4, xh, xl, z, c)


def y_down(y, xh, xl, z, c):
    return ((y + 3) % 4, xh, xl, z, c)


def x_over(y, xh, xl, z, c):
    return (y, 1 - xh, 1 - xl, z, c)


def core_over(y, xh, xl, z, c):
    return (y, xh, xl, z, 1 - c)


def pack_kernel(starts, q_ref, k_ref, v_ref, cos_ref, sin_ref, out_ref):
    cosine, sine = cos_ref[...], sin_ref[...]
    factor = math.log2(math.e) / math.sqrt(HEAD_DIM)

    def turn(block, cosine, sine):
        block = block.astype(jnp.float32)
        turned = block * cosine + pltpu.roll(block, HEAD_DIM // 2, 1) * sine
        return turned.astype(jnp.bfloat16)

    for h in range(HEADS):
        lanes = slice(h * HEAD_DIM, (h + 1) * HEAD_DIM)
        out_ref[h, 0, 0:HALF] = turn(q_ref[:, lanes], cosine * factor, sine * factor)
        out_ref[h, 0, HALF : 2 * HALF] = turn(k_ref[:, lanes], cosine, sine)
        out_ref[h, 0, 2 * HALF : 3 * HALF] = v_ref[:, lanes]
    block = jnp.full((16, HEAD_DIM), starts[pl.program_id(0)] // HALF, jnp.int32)
    block = block.astype(jnp.float32).astype(jnp.bfloat16)
    for h in range(HEADS):
        out_ref[h, 0, 3 * HALF :] = block


def pack(starts, queries, keys, values):
    cosine, sine = tables()
    rows = pl.BlockSpec((HALF, WIDTH), lambda b, s: (b, 0))
    table = pl.BlockSpec((HALF, HEAD_DIM), lambda b, s: (s[b] // HALF, 0))
    return pl.pallas_call(
        pack_kernel,
        grid_spec=pltpu.PrefetchScalarGridSpec(
            num_scalar_prefetch=1,
            grid=(2,),
            in_specs=[rows, rows, rows, table, table],
            out_specs=pl.BlockSpec((HEADS, 1, ROWS, HEAD_DIM), lambda b, s: (0, b, 0, 0)),
        ),
        out_shape=jax.ShapeDtypeStruct((HEADS, 2, ROWS, HEAD_DIM), jnp.bfloat16),
        compiler_params=pltpu.CompilerParams(vmem_limit_bytes=VMEM),
        name="pack",
    )(starts, queries, keys, values, jnp.asarray(cosine), jnp.asarray(sine))


def attention_kernel(x_ref, o_ref, qs, kt, vs, scores, index, pos, moved, *, tq, width):
    tiles = LEN // tq
    for t in range(2 * HEADS):
        row = x_ref[t // 2, t % 2, 3 * HALF :, :].astype(jnp.float32)
        index[t : t + 1, :] = row[:1].astype(jnp.int32)
    copy = pltpu.make_async_copy(index, pos, moved)
    copy.start()
    copy.wait()
    vs[:, HEAD_DIM:] = jnp.ones((LEN, HEAD_DIM), jnp.bfloat16)

    def place(t, carry):
        at = pl.ds(pl.multiple_of(pos[t, 0] * HALF, HALF), HALF)
        s, b = t // 2, t % 2
        qs[at, :] = x_ref[s, b, 0:HALF, :]
        kt[:, at] = x_ref[s, b, HALF : 2 * HALF, :].T
        vs[at, :HEAD_DIM] = x_ref[s, b, 2 * HALF : 3 * HALF, :]
        return carry

    lax.fori_loop(0, 2 * HEADS, place, 0, unroll=4)

    row = lax.broadcasted_iota(jnp.int32, (tq, tq), 0)
    col = lax.broadcasted_iota(jnp.int32, (tq, tq), 1)

    def chunks(i):
        seen = (i + 1) * tq
        return [(o, min(width, seen - o)) for o in range(0, seen, width)]

    def score(i, first, count, high):
        s = jnp.dot(
            qs[i * tq : (i + 1) * tq, :],
            kt[:, first : first + count],
            preferred_element_type=jnp.float32,
        )
        if first + count > i * tq:
            before = i * tq - first
            last = jnp.where(col <= row, s[:, before:], -1e30)
            s = jnp.concatenate([s[:, :before], last], axis=1) if before else last
        scores[i % 2, :, first : first + count] = s
        for c in range(0, count, 128):
            part = s[:, c : c + 128]
            high = part if high is None else jnp.maximum(high, part)
        return high

    def weigh(i, first, count, high, total):
        p = jnp.concatenate(
            [
                jnp.exp2(scores[i % 2, :, c : c + 128] - high).astype(jnp.bfloat16)
                for c in range(first, first + count, 128)
            ],
            axis=1,
        )
        part = jnp.dot(p, vs[first : first + count, :], preferred_element_type=jnp.float32)
        return part if total is None else total + part

    high = None
    for chunk in chunks(0):
        high = score(0, *chunk, high)
    for i in range(tiles):
        m = jnp.broadcast_to(jnp.max(high, axis=1, keepdims=True), (tq, 128))
        high = total = None
        mine, following = chunks(i), chunks(i + 1) if i + 1 < tiles else []
        for t in range(max(len(mine), len(following))):
            if t < len(following):
                high = score(i + 1, *following[t], high)
            if t < len(mine):
                total = weigh(i, *mine[t], m, total)
        qs[i * tq : (i + 1) * tq, :] = (total[:, :HEAD_DIM] / total[:, HEAD_DIM:]).astype(
            jnp.bfloat16
        )

    def unplace(t, carry):
        at = pl.ds(pl.multiple_of(pos[t, 0] * HALF, HALF), HALF)
        o_ref[t // 2, t % 2] = qs[at, :]
        return carry

    lax.fori_loop(0, 2 * HEADS, unplace, 0, unroll=4)


def attention(packed, tq=256, width=1024):
    return pl.pallas_call(
        functools.partial(attention_kernel, tq=tq, width=width),
        out_shape=jax.ShapeDtypeStruct((HEADS, 2, HALF, HEAD_DIM), jnp.bfloat16),
        in_specs=[
            pl.BlockSpec(memory_space=pltpu.VMEM),
        ],
        out_specs=pl.BlockSpec(memory_space=pltpu.VMEM),
        scratch_shapes=[
            pltpu.VMEM((LEN, HEAD_DIM), jnp.bfloat16),
            pltpu.VMEM((HEAD_DIM, LEN), jnp.bfloat16),
            pltpu.VMEM((LEN, 2 * HEAD_DIM), jnp.bfloat16),
            pltpu.VMEM((2, tq, LEN), jnp.float32),
            pltpu.VMEM((2 * HEADS, 128), jnp.int32),
            pltpu.SMEM((2 * HEADS, 128), jnp.int32),
            pltpu.SemaphoreType.DMA,
        ],
        compiler_params=pltpu.CompilerParams(vmem_limit_bytes=VMEM),
        cost_estimate=pl.CostEstimate(
            flops=8 * LEN * LEN * HEAD_DIM, bytes_accessed=4 * 2**20, transcendentals=LEN * LEN // 2
        ),
        name="attention",
    )(packed)


PIECES = ((0, 0), (0, 1), (3, 0), (1, 0), (3, 1), (1, 1), (2, 0), (2, 1))
STEP = 512
HALF_D = D // 2
GROUP = WIDTH // 2


def project_kernel(place, att_ref, hidden_ref, own_ref, *refs):
    halves = refs[:8], refs[8:16]
    out_ref, heads, left, rows, hidden, acc, out, att_sem, hidden_sem, in_sem, out_sem = refs[16:]

    def first_column(half):
        core = place[0] if half == 0 else 1 - place[0]
        return core * HALF_D

    def fetches(half):
        first, copies = 0, []
        at = pl.ds(pl.multiple_of(first_column(half), HALF_D), HALF_D)
        for n, ref in enumerate([own_ref.at[:, at], *halves[half]]):
            count = ref.shape[0]
            to = rows.at[half, first : first + count]
            copies.append((first, pltpu.make_async_copy(ref, to, in_sem.at[half, n])))
            first += count
        return copies

    att = pltpu.make_async_copy(att_ref, heads, att_sem)
    residual = pltpu.make_async_copy(hidden_ref, hidden, hidden_sem)
    pieces = [fetches(half) for half in range(2)]
    att.start()
    for first, copy in pieces[0]:
        if first == GROUP:
            residual.start()
        copy.start()
    for _, copy in pieces[1]:
        copy.start()
    att.wait()
    for n in range(len(PIECES)):
        for i in range(2):
            head = heads[2 * place[1 + n] + i].reshape(2 * HALF, HEAD_DIM)
            left[:, (2 * n + i) * HEAD_DIM : (2 * n + i + 1) * HEAD_DIM] = head
    stores = []
    for half in range(2):
        for group in range(0, WIDTH, GROUP):
            for first, copy in pieces[half]:
                if group <= first < group + GROUP:
                    copy.wait()
            if half == 0 and group > 0:
                residual.wait()
            for t in range(HALF_D // STEP):
                at = pl.ds(t * STEP, STEP)
                part = jnp.dot(
                    left[:, group : group + GROUP],
                    rows[half, group : group + GROUP, at],
                    preferred_element_type=jnp.float32,
                )
                if group == 0:
                    acc[:, at] = part
                else:
                    to = pl.ds(pl.multiple_of(first_column(half) + t * STEP, STEP), STEP)
                    total = hidden[:, to].astype(jnp.float32) + (acc[:, at] + part)
                    n = half * (HALF_D // STEP) + t
                    out[n] = total.astype(jnp.bfloat16)
                    stores.append(
                        pltpu.make_async_copy(out.at[n], out_ref.at[:, to], out_sem.at[n])
                    )
                    stores[-1].start()
    for copy in stores:
        copy.wait()


def project(place, att, hidden, own, mine, other):
    return pl.pallas_call(
        project_kernel,
        in_specs=[pl.BlockSpec(memory_space=pltpu.SMEM)]
        + [pl.BlockSpec(memory_space=pl.ANY)] * 19,
        out_specs=pl.BlockSpec(memory_space=pl.ANY),
        scratch_shapes=[
            pltpu.VMEM((HEADS, 2, HALF, HEAD_DIM), jnp.bfloat16),
            pltpu.VMEM((2 * HALF, WIDTH), jnp.bfloat16),
            pltpu.VMEM((2, WIDTH, HALF_D), jnp.bfloat16),
            pltpu.VMEM((2 * HALF, D), jnp.bfloat16),
            pltpu.VMEM((2 * HALF, HALF_D), jnp.float32),
            pltpu.VMEM((D // STEP, 2 * HALF, STEP), jnp.bfloat16),
            pltpu.SemaphoreType.DMA,
            pltpu.SemaphoreType.DMA,
            pltpu.SemaphoreType.DMA((2, 9)),
            pltpu.SemaphoreType.DMA((D // STEP,)),
        ],
        out_shape=jax.ShapeDtypeStruct((2 * HALF, D), jnp.bfloat16),
        compiler_params=pltpu.CompilerParams(vmem_limit_bytes=VMEM),
        cost_estimate=pl.CostEstimate(
            flops=4 * HALF * WIDTH * D, bytes_accessed=20 * 2**20, transcendentals=0
        ),
        name="project",
    )(place, att, hidden, own, *mine, *other)


def arrive_kernel(att_ref, out_ref):
    del att_ref, out_ref


def arrive(att):
    return pl.pallas_call(
        arrive_kernel,
        in_specs=[pl.BlockSpec(memory_space=pl.ANY)],
        out_specs=pl.BlockSpec(memory_space=pl.ANY),
        out_shape=jax.ShapeDtypeStruct(att.shape, att.dtype),
        input_output_aliases={0: 0},
        compiler_params=pltpu.CompilerParams(vmem_limit_bytes=VMEM),
        cost_estimate=pl.CostEstimate(
            flops=2 * 10**10, bytes_accessed=2 * 2**20, transcendentals=0
        ),
        name="arrive",
    )(att)


def shards(hidden_in, queries, keys, values, block_start, out_weight):
    y, xh, c = lax.axis_index("y"), lax.axis_index("xh"), lax.axis_index("c")
    packed = pack(block_start, queries[0], keys[0], values[0])
    packed = lax.all_to_all(packed, SEQ, 0, 0, tiled=True)

    half = lax.dynamic_slice(out_weight, (0, c * (D // 2)), (WIDTH // 8, D // 2))
    mine, other = {}, {}
    mine[0, 1] = send(half, x_over)
    mine[3, 0] = send(half, y_up)
    mine[1, 0] = send(half, y_down)
    second = {
        (3, 1): send(mine[3, 0], x_over),
        (1, 1): send(mine[0, 1], y_down),
        (2, 0): send(mine[3, 0], y_up),
    }
    other[0, 1] = send(mine[0, 1], core_over)
    other[3, 0] = send(mine[3, 0], core_over)
    later, _ = lax.optimization_barrier((mine[1, 0], other[3, 0]))
    other[1, 0] = send(later, core_over)

    attended = attention(packed)
    second, _ = lax.optimization_barrier((second, attended))
    attended = lax.all_to_all(attended, SEQ, 0, 0, tiled=True)
    top = send(second[3, 1][:HALF], y_up)
    bottom = send(second[1, 1][HALF:], y_down)
    last = [second[at] for at in PIECES[4:7]] + [top, bottom]
    mine = [mine[at] for at in PIECES[1:4]] + last
    other = [other[at] for at in PIECES[1:4]] + [send(a, core_over) for a in last]

    owners = [((y + dy) % 4) * 2 + (xh + dx) % 2 for dy, dx in PIECES]
    place = jnp.stack([c, *owners]).astype(jnp.int32)
    attended = arrive(attended)
    return project(place, attended, hidden_in[0], out_weight, mine, other)[None]


def solution(mesh):
    fine = Mesh(mesh.devices.reshape(SIZES), AXES)
    return jax.shard_map(
        shards,
        mesh=fine,
        in_specs=(
            P(FSDP, SEQ, None),
            P(FSDP, SEQ, None),
            P(FSDP, SEQ, None),
            P(FSDP, SEQ, None),
            P(SEQ),
            P(FSDP, None),
        ),
        out_specs=P(FSDP, SEQ, None),
        check_vma=False,
    )
```

```python
import functools
import itertools
import math

import jax
import jax.numpy as jnp
import numpy as np
from jax import lax
from jax.experimental import pallas as pl
from jax.experimental.pallas import tpu as pltpu
from jax.sharding import Mesh
from jax.sharding import PartitionSpec as P

HEADS = 16
HEAD_DIM = 128
LEN = 4096
HALF = 128
WIDTH = HEADS * HEAD_DIM
D = 4096
ROWS = 3 * HALF + 16
AXES = ("y", "xh", "xl", "z", "c")
SIZES = (4, 2, 2, 4, 2)
FSDP = ("y", "xh")
SEQ = ("xl", "z", "c")
VMEM = 56 * 2**20
SMALL = 24 * 2**20


def tables():
    frequency = 10000.0 ** (-np.arange(HEAD_DIM // 2) / (HEAD_DIM // 2))
    angles = np.arange(LEN)[:, None] * frequency[None, :]
    cosine, sine = np.cos(angles), np.sin(angles)
    return (
        np.concatenate([cosine, cosine], axis=1).astype(np.float32),
        np.concatenate([-sine, sine], axis=1).astype(np.float32),
    )


def send(array, move):
    places = list(itertools.product(*map(range, SIZES)))
    index = {place: i for i, place in enumerate(places)}
    return lax.ppermute(array, AXES, [(index[p], index[move(*p)]) for p in places])


def y_up(y, xh, xl, z, c):
    return ((y + 1) % 4, xh, xl, z, c)


def y_down(y, xh, xl, z, c):
    return ((y + 3) % 4, xh, xl, z, c)


def x_over(y, xh, xl, z, c):
    return (y, 1 - xh, 1 - xl, z, c)


def x_over_y_down(y, xh, xl, z, c):
    return ((y + 3) % 4, 1 - xh, 1 - xl, z, c)


def core_over(y, xh, xl, z, c):
    return (y, xh, xl, z, 1 - c)


def pack_kernel(starts, q_ref, k_ref, v_ref, cos_ref, sin_ref, out_ref):
    cosine, sine = cos_ref[...], sin_ref[...]
    factor = math.log2(math.e) / math.sqrt(HEAD_DIM)

    def turn(block, cosine, sine):
        block = block.astype(jnp.float32)
        turned = block * cosine + pltpu.roll(block, HEAD_DIM // 2, 1) * sine
        return turned.astype(jnp.bfloat16)

    for h in range(HEADS):
        lanes = slice(h * HEAD_DIM, (h + 1) * HEAD_DIM)
        out_ref[h, 0, 0:HALF] = turn(q_ref[:, lanes], cosine * factor, sine * factor)
        out_ref[h, 0, HALF : 2 * HALF] = turn(k_ref[:, lanes], cosine, sine)
        out_ref[h, 0, 2 * HALF : 3 * HALF] = v_ref[:, lanes]
    block = jnp.full((16, HEAD_DIM), starts[pl.program_id(0)] // HALF, jnp.int32)
    block = block.astype(jnp.float32).astype(jnp.bfloat16)
    for h in range(HEADS):
        out_ref[h, 0, 3 * HALF :] = block


def pack(starts, queries, keys, values):
    cosine, sine = tables()
    rows = pl.BlockSpec((HALF, WIDTH), lambda b, s: (b, 0))
    table = pl.BlockSpec((HALF, HEAD_DIM), lambda b, s: (s[b] // HALF, 0))
    return pl.pallas_call(
        pack_kernel,
        grid_spec=pltpu.PrefetchScalarGridSpec(
            num_scalar_prefetch=1,
            grid=(2,),
            in_specs=[rows, rows, rows, table, table],
            out_specs=pl.BlockSpec((HEADS, 1, ROWS, HEAD_DIM), lambda b, s: (0, b, 0, 0)),
        ),
        out_shape=jax.ShapeDtypeStruct((HEADS, 2, ROWS, HEAD_DIM), jnp.bfloat16),
        compiler_params=pltpu.CompilerParams(vmem_limit_bytes=VMEM),
        name="pack",
    )(starts, queries, keys, values, jnp.asarray(cosine), jnp.asarray(sine))


def attention_kernel(x_ref, o_ref, qs, kt, vs, scores, index, pos, moved, left, *, tq, width):
    tiles = LEN // tq
    for t in range(2 * HEADS):
        row = x_ref[t // 2, t % 2, 3 * HALF :, :].astype(jnp.float32)
        index[t : t + 1, :] = row[:1].astype(jnp.int32)
    copy = pltpu.make_async_copy(index, pos, moved)
    copy.start()
    copy.wait()
    vs[:, HEAD_DIM:] = jnp.ones((LEN, HEAD_DIM), jnp.bfloat16)

    def place(t, carry):
        at = pl.ds(pl.multiple_of(pos[t, 0] * HALF, HALF), HALF)
        s, b = t // 2, t % 2
        qs[at, :] = x_ref[s, b, 0:HALF, :]
        kt[:, at] = x_ref[s, b, HALF : 2 * HALF, :].T
        vs[at, :HEAD_DIM] = x_ref[s, b, 2 * HALF : 3 * HALF, :]
        return carry

    lax.fori_loop(0, 2 * HEADS, place, 0, unroll=4)

    row = lax.broadcasted_iota(jnp.int32, (tq, tq), 0)
    col = lax.broadcasted_iota(jnp.int32, (tq, tq), 1)

    def chunks(i):
        seen = (i + 1) * tq
        return [(o, min(width, seen - o)) for o in range(0, seen, width)]

    def score(i, first, count, high):
        s = jnp.dot(
            qs[i * tq : (i + 1) * tq, :],
            kt[:, first : first + count],
            preferred_element_type=jnp.float32,
        )
        if first + count > i * tq:
            before = i * tq - first
            last = jnp.where(col <= row, s[:, before:], -1e30)
            s = jnp.concatenate([s[:, :before], last], axis=1) if before else last
        scores[i % 2, :, first : first + count] = s
        for c in range(0, count, 128):
            part = s[:, c : c + 128]
            high = part if high is None else jnp.maximum(high, part)
        return high

    def weigh(i, first, count, high, total):
        p = jnp.concatenate(
            [
                jnp.exp2(scores[i % 2, :, c : c + 128] - high).astype(jnp.bfloat16)
                for c in range(first, first + count, 128)
            ],
            axis=1,
        )
        part = jnp.dot(p, vs[first : first + count, :], preferred_element_type=jnp.float32)
        return part if total is None else total + part

    high = None
    for chunk in chunks(0):
        high = score(0, *chunk, high)
    for i in range(tiles):
        m = jnp.broadcast_to(jnp.max(high, axis=1, keepdims=True), (tq, 128))
        high = total = None
        mine, following = chunks(i), chunks(i + 1) if i + 1 < tiles else []
        for t in range(max(len(mine), len(following))):
            if t < len(following):
                high = score(i + 1, *following[t], high)
            if t < len(mine):
                total = weigh(i, *mine[t], m, total)
        qs[i * tq : (i + 1) * tq, :] = (total[:, :HEAD_DIM] / total[:, HEAD_DIM:]).astype(
            jnp.bfloat16
        )

    def leave(t):
        from_ = qs.at[pl.ds(pl.multiple_of(pos[t, 0] * HALF, HALF), HALF)]
        return pltpu.make_async_copy(from_, o_ref.at[t // 2, t % 2], left.at[t])

    def start(t, carry):
        leave(t).start()
        return carry

    def wait(t, carry):
        leave(t).wait()
        return carry

    lax.fori_loop(0, 2 * HEADS, start, 0, unroll=8)
    lax.fori_loop(0, 2 * HEADS, wait, 0, unroll=8)


def attention(packed, tq=256, width=1024):
    return pl.pallas_call(
        functools.partial(attention_kernel, tq=tq, width=width),
        out_shape=pltpu.HBM((HEADS, 2, HALF, HEAD_DIM), jnp.bfloat16),
        in_specs=[
            pl.BlockSpec(memory_space=pltpu.VMEM),
        ],
        out_specs=pl.BlockSpec(memory_space=pltpu.HBM),
        scratch_shapes=[
            pltpu.VMEM((LEN, HEAD_DIM), jnp.bfloat16),
            pltpu.VMEM((HEAD_DIM, LEN), jnp.bfloat16),
            pltpu.VMEM((LEN, 2 * HEAD_DIM), jnp.bfloat16),
            pltpu.VMEM((2, tq, LEN), jnp.float32),
            pltpu.VMEM((2 * HEADS, 128), jnp.int32),
            pltpu.SMEM((2 * HEADS, 128), jnp.int32),
            pltpu.SemaphoreType.DMA,
            pltpu.SemaphoreType.DMA((2 * HEADS,)),
        ],
        compiler_params=pltpu.CompilerParams(vmem_limit_bytes=SMALL),
        cost_estimate=pl.CostEstimate(
            flops=8 * LEN * LEN * HEAD_DIM, bytes_accessed=4 * 2**20, transcendentals=LEN * LEN // 2
        ),
        name="attention",
    )(packed)


PIECES = ((0, 0), (0, 1), (3, 0), (1, 0), (3, 1), (1, 1), (2, 0), (2, 1))
STEP = 512
HALF_D = D // 2
GROUP = WIDTH // 4


def project_kernel(place, att_ref, hidden_ref, own_ref, *refs, half):
    pieces = refs[:7]
    out_ref, heads, left, rows, hidden, acc, out, att_sem, hidden_sem, in_sem, out_sem = refs[-11:]
    core = place[0] if half == 0 else 1 - place[0]
    here = pl.ds(pl.multiple_of(core * HALF_D, HALF_D), HALF_D)
    first, fetches = 0, []
    for n, ref in enumerate([own_ref.at[:, here], *pieces]):
        to = rows.at[first : first + ref.shape[0]]
        fetches.append((first, pltpu.make_async_copy(ref, to, in_sem.at[n])))
        first += ref.shape[0]
    att = pltpu.make_async_copy(att_ref, heads, att_sem)
    residual = pltpu.make_async_copy(hidden_ref.at[:, here], hidden, hidden_sem)
    att.start()
    for _, copy in fetches:
        copy.start()
    residual.start()
    att.wait()
    for n in range(len(PIECES)):
        for i in range(2):
            head = heads[2 * place[1 + n] + i].reshape(2 * HALF, HEAD_DIM)
            left[:, (2 * n + i) * HEAD_DIM : (2 * n + i + 1) * HEAD_DIM] = head
    stores = []
    for group in range(0, WIDTH, GROUP):
        for first, copy in fetches:
            if group <= first < group + GROUP:
                copy.wait()
        if group + GROUP == WIDTH:
            residual.wait()
        for t in range(HALF_D // STEP):
            at = pl.ds(t * STEP, STEP)
            part = jnp.dot(
                left[:, group : group + GROUP],
                rows[group : group + GROUP, at],
                preferred_element_type=jnp.float32,
            )
            if group > 0:
                part += acc[:, at]
            if group + GROUP < WIDTH:
                acc[:, at] = part
            else:
                out[t] = (hidden[:, at].astype(jnp.float32) + part).astype(jnp.bfloat16)
                to = pl.ds(pl.multiple_of(core * HALF_D + t * STEP, STEP), STEP)
                store = pltpu.make_async_copy(out.at[t], out_ref.at[:, to], out_sem.at[t])
                store.start()
                stores.append(store)
    for store in stores:
        store.wait()


def project(half, place, att, hidden, own, pieces, *done):
    hidden = pltpu.with_memory_space_constraint(hidden, pltpu.HBM)
    return pl.pallas_call(
        functools.partial(project_kernel, half=half),
        in_specs=[pl.BlockSpec(memory_space=pltpu.SMEM)]
        + [pl.BlockSpec(memory_space=pl.ANY)] * (10 + len(done)),
        out_specs=pl.BlockSpec(memory_space=pl.ANY),
        scratch_shapes=[
            pltpu.VMEM((HEADS, 2, HALF, HEAD_DIM), jnp.bfloat16),
            pltpu.VMEM((2 * HALF, WIDTH), jnp.bfloat16),
            pltpu.VMEM((WIDTH, HALF_D), jnp.bfloat16),
            pltpu.VMEM((2 * HALF, HALF_D), jnp.bfloat16),
            pltpu.VMEM((2 * HALF, HALF_D), jnp.float32),
            pltpu.VMEM((HALF_D // STEP, 2 * HALF, STEP), jnp.bfloat16),
            pltpu.SemaphoreType.DMA,
            pltpu.SemaphoreType.DMA,
            pltpu.SemaphoreType.DMA((8,)),
            pltpu.SemaphoreType.DMA((HALF_D // STEP,)),
        ],
        out_shape=jax.ShapeDtypeStruct((2 * HALF, D), jnp.bfloat16),
        input_output_aliases={11: 0} if done else {},
        compiler_params=pltpu.CompilerParams(vmem_limit_bytes=SMALL),
        cost_estimate=pl.CostEstimate(
            flops=2 * HALF * WIDTH * D, bytes_accessed=12 * 2**20, transcendentals=0
        ),
        name="project",
    )(place, att, hidden, own, *pieces, *done)


def arrive_kernel(att_ref, out_ref):
    del att_ref, out_ref


def arrive(att):
    return pl.pallas_call(
        arrive_kernel,
        in_specs=[pl.BlockSpec(memory_space=pl.ANY)],
        out_specs=pl.BlockSpec(memory_space=pl.ANY),
        out_shape=jax.ShapeDtypeStruct(att.shape, att.dtype),
        input_output_aliases={0: 0},
        compiler_params=pltpu.CompilerParams(vmem_limit_bytes=SMALL),
        cost_estimate=pl.CostEstimate(
            flops=2 * 10**10, bytes_accessed=2 * 2**20, transcendentals=0
        ),
        name="arrive",
    )(att)


def shards(hidden_in, queries, keys, values, block_start, out_weight):
    y, xh, c = lax.axis_index("y"), lax.axis_index("xh"), lax.axis_index("c")
    packed = pack(block_start, queries[0], keys[0], values[0])
    packed = lax.all_to_all(packed, SEQ, 0, 0, tiled=True)

    half = lax.dynamic_slice(out_weight, (0, c * (D // 2)), (WIDTH // 8, D // 2))
    mine, other = {}, {}
    mine[0, 1] = send(half, x_over)
    mine[3, 0] = send(half, y_up)
    mine[1, 0] = send(half, y_down)
    second = {
        (3, 1): send(mine[3, 0], x_over),
        (1, 1): send(mine[0, 1], y_down),
        (2, 0): send(mine[3, 0], y_up),
        (2, 1): send(mine[1, 0], x_over_y_down),
    }
    before = mine[3, 0]
    for at in (3, 0), (0, 1), (1, 0):
        piece, _ = lax.optimization_barrier((mine[at], before))
        other[at] = before = send(piece, core_over)

    attended = attention(packed)
    second, _ = lax.optimization_barrier((second, attended))
    attended = lax.all_to_all(attended, SEQ, 0, 0, tiled=True)
    for at in second:
        mine[at] = second[at]
        other[at] = send(mine[at], core_over)
    mine = [mine[at] for at in PIECES[1:]]
    other = [other[at] for at in PIECES[1:]]

    owners = [((y + dy) % 4) * 2 + (xh + dx) % 2 for dy, dx in PIECES]
    place = jnp.stack([c, *owners]).astype(jnp.int32)
    attended = arrive(attended)
    done = project(0, place, attended, hidden_in[0], out_weight, mine)
    return project(1, place, attended, hidden_in[0], out_weight, other, done)[None]


def solution(mesh):
    fine = Mesh(mesh.devices.reshape(SIZES), AXES)
    return jax.shard_map(
        shards,
        mesh=fine,
        in_specs=(
            P(FSDP, SEQ, None),
            P(FSDP, SEQ, None),
            P(FSDP, SEQ, None),
            P(FSDP, SEQ, None),
            P(SEQ),
            P(FSDP, None),
        ),
        out_specs=P(FSDP, SEQ, None),
        check_vma=False,
    )
```

```python
import functools
import itertools
import math

import jax
import jax.numpy as jnp
import numpy as np
from jax import lax
from jax.experimental import pallas as pl
from jax.experimental.pallas import tpu as pltpu
from jax.sharding import Mesh
from jax.sharding import PartitionSpec as P

HEADS = 16
HEAD_DIM = 128
LEN = 4096
HALF = 128
WIDTH = HEADS * HEAD_DIM
D = 4096
ROWS = 3 * HALF + 16
AXES = ("y", "xh", "xl", "z", "c")
SIZES = (4, 2, 2, 4, 2)
FSDP = ("y", "xh")
SEQ = ("xl", "z", "c")
OWNERS = ("z", "c", "xl")
VMEM = 56 * 2**20
SMALL = 24 * 2**20


def tables():
    frequency = 10000.0 ** (-np.arange(HEAD_DIM // 2) / (HEAD_DIM // 2))
    angles = np.arange(LEN)[:, None] * frequency[None, :]
    cosine, sine = np.cos(angles), np.sin(angles)
    return (
        np.concatenate([cosine, cosine], axis=1).astype(np.float32),
        np.concatenate([-sine, sine], axis=1).astype(np.float32),
    )


def send(array, move):
    places = list(itertools.product(*map(range, SIZES)))
    index = {place: i for i, place in enumerate(places)}
    return lax.ppermute(array, AXES, [(index[p], index[move(*p)]) for p in places])


def y_up(y, xh, xl, z, c):
    return ((y + 1) % 4, xh, xl, z, c)


def y_down(y, xh, xl, z, c):
    return ((y + 3) % 4, xh, xl, z, c)


def x_over(y, xh, xl, z, c):
    return (y, 1 - xh, 1 - xl, z, c)


def x_over_y_down(y, xh, xl, z, c):
    return ((y + 3) % 4, 1 - xh, 1 - xl, z, c)


def core_over(y, xh, xl, z, c):
    return (y, xh, xl, z, 1 - c)


def pack_kernel(starts, q_ref, k_ref, v_ref, cos_ref, sin_ref, out_ref, *scratch):
    q, k, v, cosine, sine, turned, index, in_sem, out_sem = scratch
    factor = math.log2(math.e) / math.sqrt(HEAD_DIM)
    fetches = []
    for b in range(2):
        rows = pl.ds(b * HALF, HALF)
        at = pl.ds(pl.multiple_of(starts[b], HALF), HALF)
        pairs = [
            (cos_ref.at[at], cosine.at[b]),
            (sin_ref.at[at], sine.at[b]),
            (q_ref.at[rows], q.at[b]),
            (k_ref.at[rows], k.at[b]),
            (v_ref.at[rows], v.at[b]),
        ]
        fetches.append(
            [
                pltpu.make_async_copy(source, target, in_sem.at[b, n])
                for n, (source, target) in enumerate(pairs)
            ]
        )
    for copies in fetches:
        for copy in copies:
            copy.start()

    stores = []

    def leave(source, target):
        copy = pltpu.make_async_copy(source, target, out_sem.at[len(stores)])
        copy.start()
        stores.append(copy)

    def turn(block, cosine, sine):
        block = block.astype(jnp.float32)
        rolled = pltpu.roll(block, HEAD_DIM // 2, 1)
        return (block * cosine + rolled * sine).astype(jnp.bfloat16)

    for b in range(2):
        block = jnp.full((16, HEAD_DIM), starts[b] // HALF, jnp.int32)
        block = block.astype(jnp.float32).astype(jnp.bfloat16)
        for h in range(HEADS):
            index[h, b] = block
    leave(index, out_ref.at[:, :, 3 * HALF :])
    for b in range(2):
        for copy in fetches[b]:
            copy.wait()
        for h in range(HEADS):
            lanes = pl.ds(h * HEAD_DIM, HEAD_DIM)
            leave(v.at[b, :, lanes], out_ref.at[h, b, 2 * HALF : 3 * HALF])
        for part, source, scale in (0, q, factor), (1, k, 1.0):
            cos_b, sin_b = cosine[b] * scale, sine[b] * scale
            for h in range(HEADS):
                lanes = slice(h * HEAD_DIM, (h + 1) * HEAD_DIM)
                turned[b, part, h] = turn(source[b, :, lanes], cos_b, sin_b)
            leave(turned.at[b, part], out_ref.at[:, b, part * HALF : (part + 1) * HALF])
    for copy in stores:
        copy.wait()


def pack(starts, queries, keys, values):
    cosine, sine = tables()
    anywhere = pl.BlockSpec(memory_space=pl.ANY)
    rows = pltpu.VMEM((2, HALF, WIDTH), jnp.bfloat16)
    table = pltpu.VMEM((2, HALF, HEAD_DIM), jnp.float32)
    return pl.pallas_call(
        pack_kernel,
        in_specs=[pl.BlockSpec(memory_space=pltpu.SMEM)] + [anywhere] * 5,
        out_specs=anywhere,
        scratch_shapes=[
            rows,
            rows,
            rows,
            table,
            table,
            pltpu.VMEM((2, 2, HEADS, HALF, HEAD_DIM), jnp.bfloat16),
            pltpu.VMEM((HEADS, 2, 16, HEAD_DIM), jnp.bfloat16),
            pltpu.SemaphoreType.DMA((2, 5)),
            pltpu.SemaphoreType.DMA((1 + 2 * (HEADS + 2),)),
        ],
        out_shape=jax.ShapeDtypeStruct((HEADS, 2, ROWS, HEAD_DIM), jnp.bfloat16),
        compiler_params=pltpu.CompilerParams(vmem_limit_bytes=VMEM),
        name="pack",
    )(starts, queries, keys, values, jnp.asarray(cosine), jnp.asarray(sine))


def attention_kernel(packed, o_ref, x_ref, qs, kt, vs, scores, index, pos, got, moved, left, *, tq, width):
    tiles = LEN // tq
    fetches = [
        pltpu.make_async_copy(packed.at[:, :, 3 * HALF :], x_ref.at[:, :, 3 * HALF :], got.at[0]),
        *[
            pltpu.make_async_copy(packed.at[s, :, : 3 * HALF], x_ref.at[s, :, : 3 * HALF], got.at[1 + s])
            for s in range(HEADS)
        ],
    ]
    for fetch in fetches:
        fetch.start()
    vs[:, HEAD_DIM:] = jnp.ones((LEN, HEAD_DIM), jnp.bfloat16)
    fetches[0].wait()
    for t in range(2 * HEADS):
        row = x_ref[t // 2, t % 2, 3 * HALF :, :].astype(jnp.float32)
        index[t : t + 1, :] = row[:1].astype(jnp.int32)
    copy = pltpu.make_async_copy(index, pos, moved)
    copy.start()
    copy.wait()
    for fetch in fetches[1:]:
        fetch.wait()

    def place(t, carry):
        at = pl.ds(pl.multiple_of(pos[t, 0] * HALF, HALF), HALF)
        s, b = t // 2, t % 2
        qs[at, :] = x_ref[s, b, 0:HALF, :]
        kt[:, at] = x_ref[s, b, HALF : 2 * HALF, :].T
        vs[at, :HEAD_DIM] = x_ref[s, b, 2 * HALF : 3 * HALF, :]
        return carry

    lax.fori_loop(0, 2 * HEADS, place, 0, unroll=4)

    row = lax.broadcasted_iota(jnp.int32, (tq, tq), 0)
    col = lax.broadcasted_iota(jnp.int32, (tq, tq), 1)

    def chunks(i):
        seen = (i + 1) * tq
        return [(o, min(width, seen - o)) for o in range(0, seen, width)]

    def score(i, first, count, high):
        s = jnp.dot(
            qs[i * tq : (i + 1) * tq, :],
            kt[:, first : first + count],
            preferred_element_type=jnp.float32,
        )
        if first + count > i * tq:
            before = i * tq - first
            last = jnp.where(col <= row, s[:, before:], -1e30)
            s = jnp.concatenate([s[:, :before], last], axis=1) if before else last
        scores[i % 2, :, first : first + count] = s
        for c in range(0, count, 128):
            part = s[:, c : c + 128]
            high = part if high is None else jnp.maximum(high, part)
        return high

    def weigh(i, first, count, high, total):
        p = jnp.concatenate(
            [
                jnp.exp2(scores[i % 2, :, c : c + 128] - high).astype(jnp.bfloat16)
                for c in range(first, first + count, 128)
            ],
            axis=1,
        )
        part = jnp.dot(p, vs[first : first + count, :], preferred_element_type=jnp.float32)
        return part if total is None else total + part

    high = None
    for chunk in chunks(0):
        high = score(0, *chunk, high)
    for i in range(tiles):
        m = jnp.broadcast_to(jnp.max(high, axis=1, keepdims=True), (tq, 128))
        high = total = None
        mine, following = chunks(i), chunks(i + 1) if i + 1 < tiles else []
        for t in range(max(len(mine), len(following))):
            if t < len(following):
                high = score(i + 1, *following[t], high)
            if t < len(mine):
                total = weigh(i, *mine[t], m, total)
        qs[i * tq : (i + 1) * tq, :] = (total[:, :HEAD_DIM] / total[:, HEAD_DIM:]).astype(
            jnp.bfloat16
        )

    def leave(t):
        from_ = qs.at[pl.ds(pl.multiple_of(pos[t, 0] * HALF, HALF), HALF)]
        return pltpu.make_async_copy(from_, o_ref.at[t // 2, t % 2], left.at[t])

    def start(t, carry):
        leave(t).start()
        return carry

    def wait(t, carry):
        leave(t).wait()
        return carry

    lax.fori_loop(0, 2 * HEADS, start, 0, unroll=8)
    lax.fori_loop(0, 2 * HEADS, wait, 0, unroll=8)


def attention(packed, tq=256, width=1024):
    return pl.pallas_call(
        functools.partial(attention_kernel, tq=tq, width=width),
        out_shape=pltpu.HBM((HEADS, 2, HALF, HEAD_DIM), jnp.bfloat16),
        in_specs=[
            pl.BlockSpec(memory_space=pl.ANY),
        ],
        out_specs=pl.BlockSpec(memory_space=pltpu.HBM),
        scratch_shapes=[
            pltpu.VMEM((HEADS, 2, ROWS, HEAD_DIM), jnp.bfloat16),
            pltpu.VMEM((LEN, HEAD_DIM), jnp.bfloat16),
            pltpu.VMEM((HEAD_DIM, LEN), jnp.bfloat16),
            pltpu.VMEM((LEN, 2 * HEAD_DIM), jnp.bfloat16),
            pltpu.VMEM((2, tq, LEN), jnp.float32),
            pltpu.VMEM((2 * HEADS, 128), jnp.int32),
            pltpu.SMEM((2 * HEADS, 128), jnp.int32),
            pltpu.SemaphoreType.DMA((1 + HEADS,)),
            pltpu.SemaphoreType.DMA,
            pltpu.SemaphoreType.DMA((2 * HEADS,)),
        ],
        compiler_params=pltpu.CompilerParams(vmem_limit_bytes=SMALL),
        cost_estimate=pl.CostEstimate(
            flops=8 * LEN * LEN * HEAD_DIM, bytes_accessed=4 * 2**20, transcendentals=LEN * LEN // 2
        ),
        name="attention",
    )(packed)


PIECES = ((0, 0), (0, 1), (3, 0), (1, 0), (3, 1), (1, 1), (2, 0), (2, 1))
STEP = 512
HALF_D = D // 2
GROUP = WIDTH // 4


def project_kernel(place, att_ref, hidden_ref, own_ref, *refs, half):
    pieces = refs[:7]
    out_ref, heads, left, rows, hidden, acc, out, att_sem, hidden_sem, in_sem, out_sem = refs[-11:]
    core = place[0] if half == 0 else 1 - place[0]
    here = pl.ds(pl.multiple_of(core * HALF_D, HALF_D), HALF_D)
    first, fetches = 0, []
    for n, ref in enumerate([own_ref.at[:, here], *pieces]):
        to = rows.at[first : first + ref.shape[0]]
        fetches.append((first, pltpu.make_async_copy(ref, to, in_sem.at[n])))
        first += ref.shape[0]
    att = pltpu.make_async_copy(att_ref, heads, att_sem)
    residual = pltpu.make_async_copy(hidden_ref.at[:, here], hidden, hidden_sem)
    att.start()
    for _, copy in fetches:
        copy.start()
    residual.start()
    att.wait()
    for n in range(len(PIECES)):
        for i in range(2):
            head = heads[2 * place[1 + n] + i].reshape(2 * HALF, HEAD_DIM)
            left[:, (2 * n + i) * HEAD_DIM : (2 * n + i + 1) * HEAD_DIM] = head
    stores = []
    for group in range(0, WIDTH, GROUP):
        for first, copy in fetches:
            if group <= first < group + GROUP:
                copy.wait()
        if group + GROUP == WIDTH:
            residual.wait()
        for t in range(HALF_D // STEP):
            at = pl.ds(t * STEP, STEP)
            part = jnp.dot(
                left[:, group : group + GROUP],
                rows[group : group + GROUP, at],
                preferred_element_type=jnp.float32,
            )
            if group > 0:
                part += acc[:, at]
            if group + GROUP < WIDTH:
                acc[:, at] = part
            else:
                out[t] = (hidden[:, at].astype(jnp.float32) + part).astype(jnp.bfloat16)
                to = pl.ds(pl.multiple_of(core * HALF_D + t * STEP, STEP), STEP)
                store = pltpu.make_async_copy(out.at[t], out_ref.at[:, to], out_sem.at[t])
                store.start()
                stores.append(store)
    for store in stores:
        store.wait()


def project(half, place, att, hidden, own, pieces, *done):
    hidden = pltpu.with_memory_space_constraint(hidden, pltpu.HBM)
    return pl.pallas_call(
        functools.partial(project_kernel, half=half),
        in_specs=[pl.BlockSpec(memory_space=pltpu.SMEM)]
        + [pl.BlockSpec(memory_space=pl.ANY)] * (10 + len(done)),
        out_specs=pl.BlockSpec(memory_space=pl.ANY),
        scratch_shapes=[
            pltpu.VMEM((HEADS, 2, HALF, HEAD_DIM), jnp.bfloat16),
            pltpu.VMEM((2 * HALF, WIDTH), jnp.bfloat16),
            pltpu.VMEM((WIDTH, HALF_D), jnp.bfloat16),
            pltpu.VMEM((2 * HALF, HALF_D), jnp.bfloat16),
            pltpu.VMEM((2 * HALF, HALF_D), jnp.float32),
            pltpu.VMEM((HALF_D // STEP, 2 * HALF, STEP), jnp.bfloat16),
            pltpu.SemaphoreType.DMA,
            pltpu.SemaphoreType.DMA,
            pltpu.SemaphoreType.DMA((8,)),
            pltpu.SemaphoreType.DMA((HALF_D // STEP,)),
        ],
        out_shape=jax.ShapeDtypeStruct((2 * HALF, D), jnp.bfloat16),
        input_output_aliases={11: 0} if done else {},
        compiler_params=pltpu.CompilerParams(vmem_limit_bytes=SMALL),
        cost_estimate=pl.CostEstimate(
            flops=2 * HALF * WIDTH * D, bytes_accessed=12 * 2**20, transcendentals=0
        ),
        name="project",
    )(place, att, hidden, own, *pieces, *done)


def arrive_kernel(att_ref, out_ref):
    del att_ref, out_ref


def arrive(att):
    return pl.pallas_call(
        arrive_kernel,
        in_specs=[pl.BlockSpec(memory_space=pl.ANY)],
        out_specs=pl.BlockSpec(memory_space=pl.ANY),
        out_shape=jax.ShapeDtypeStruct(att.shape, att.dtype),
        input_output_aliases={0: 0},
        compiler_params=pltpu.CompilerParams(vmem_limit_bytes=SMALL),
        cost_estimate=pl.CostEstimate(
            flops=2 * 10**10, bytes_accessed=2 * 2**20, transcendentals=0
        ),
        name="arrive",
    )(att)


def shards(hidden_in, queries, keys, values, block_start, out_weight):
    y, xh, c = lax.axis_index("y"), lax.axis_index("xh"), lax.axis_index("c")
    packed = pack(block_start, queries[0], keys[0], values[0])
    packed = lax.all_to_all(packed, OWNERS, 0, 0, tiled=True)

    half = lax.dynamic_slice(out_weight, (0, c * (D // 2)), (WIDTH // 8, D // 2))
    mine, other = {}, {}
    mine[0, 1] = send(half, x_over)
    mine[3, 0] = send(half, y_up)
    mine[1, 0] = send(half, y_down)
    second = {
        (3, 1): send(mine[3, 0], x_over),
        (1, 1): send(mine[0, 1], y_down),
        (2, 0): send(mine[3, 0], y_up),
        (2, 1): send(mine[1, 0], x_over_y_down),
    }
    before = mine[3, 0]
    for at in (3, 0), (0, 1), (1, 0):
        piece, _ = lax.optimization_barrier((mine[at], before))
        other[at] = before = send(piece, core_over)

    attended = attention(packed)
    second, _ = lax.optimization_barrier((second, attended))
    attended = lax.all_to_all(attended, OWNERS, 0, 0, tiled=True)
    for at in second:
        mine[at] = second[at]
        other[at] = send(mine[at], core_over)
    mine = [mine[at] for at in PIECES[1:]]
    other = [other[at] for at in PIECES[1:]]

    owners = [((y + dy) % 4) * 2 + (xh + dx) % 2 for dy, dx in PIECES]
    place = jnp.stack([c, *owners]).astype(jnp.int32)
    attended = arrive(attended)
    done = project(0, place, attended, hidden_in[0], out_weight, mine)
    return project(1, place, attended, hidden_in[0], out_weight, other, done)[None]


def solution(mesh):
    fine = Mesh(mesh.devices.reshape(SIZES), AXES)
    return jax.shard_map(
        shards,
        mesh=fine,
        in_specs=(
            P(FSDP, SEQ, None),
            P(FSDP, SEQ, None),
            P(FSDP, SEQ, None),
            P(FSDP, SEQ, None),
            P(SEQ),
            P(FSDP, None),
        ),
        out_specs=P(FSDP, SEQ, None),
        check_vma=False,
    )
```

```python
import functools
import itertools
import math

import jax
import jax.numpy as jnp
import numpy as np
from jax import lax
from jax.experimental import pallas as pl
from jax.experimental.pallas import tpu as pltpu
from jax.sharding import Mesh
from jax.sharding import PartitionSpec as P

HEADS = 16
HEAD_DIM = 128
LEN = 4096
HALF = 128
WIDTH = HEADS * HEAD_DIM
D = 4096
ROWS = 3 * HALF + 16
AXES = ("y", "xh", "xl", "z", "c")
SIZES = (4, 2, 2, 4, 2)
FSDP = ("y", "xh")
SEQ = ("xl", "z", "c")
OWNERS = ("z", "c", "xl")
VMEM = 56 * 2**20
SMALL = 24 * 2**20


def tables():
    frequency = 10000.0 ** (-np.arange(HEAD_DIM // 2) / (HEAD_DIM // 2))
    angles = np.arange(LEN)[:, None] * frequency[None, :]
    cosine, sine = np.cos(angles), np.sin(angles)
    return (
        np.concatenate([cosine, cosine], axis=1).astype(np.float32),
        np.concatenate([-sine, sine], axis=1).astype(np.float32),
    )


def send(array, move):
    places = list(itertools.product(*map(range, SIZES)))
    index = {place: i for i, place in enumerate(places)}
    return lax.ppermute(array, AXES, [(index[p], index[move(*p)]) for p in places])


def y_up(y, xh, xl, z, c):
    return ((y + 1) % 4, xh, xl, z, c)


def y_down(y, xh, xl, z, c):
    return ((y + 3) % 4, xh, xl, z, c)


def x_over(y, xh, xl, z, c):
    return (y, 1 - xh, 1 - xl, z, c)


def x_over_y_down(y, xh, xl, z, c):
    return ((y + 3) % 4, 1 - xh, 1 - xl, z, c)


def core_over(y, xh, xl, z, c):
    return (y, xh, xl, z, 1 - c)


def pack_kernel(starts, q_ref, k_ref, v_ref, cos_ref, sin_ref, out_ref, *scratch):
    q, k, v, cosine, sine, turned, index, in_sem, out_sem = scratch
    factor = math.log2(math.e) / math.sqrt(HEAD_DIM)
    fetches = []
    for b in range(2):
        rows = pl.ds(b * HALF, HALF)
        at = pl.ds(pl.multiple_of(starts[b], HALF), HALF)
        pairs = [
            (cos_ref.at[at], cosine.at[b]),
            (sin_ref.at[at], sine.at[b]),
            (q_ref.at[rows], q.at[b]),
            (k_ref.at[rows], k.at[b]),
            (v_ref.at[rows], v.at[b]),
        ]
        fetches.append(
            [
                pltpu.make_async_copy(source, target, in_sem.at[b, n])
                for n, (source, target) in enumerate(pairs)
            ]
        )
    for copies in fetches:
        for copy in copies:
            copy.start()

    stores = []

    def leave(source, target):
        copy = pltpu.make_async_copy(source, target, out_sem.at[len(stores)])
        copy.start()
        stores.append(copy)

    def turn(block, cosine, sine):
        block = block.astype(jnp.float32)
        rolled = pltpu.roll(block, HEAD_DIM // 2, 1)
        return (block * cosine + rolled * sine).astype(jnp.bfloat16)

    for b in range(2):
        block = jnp.full((16, HEAD_DIM), starts[b] // HALF, jnp.int32)
        block = block.astype(jnp.float32).astype(jnp.bfloat16)
        for h in range(HEADS):
            index[h, b] = block
    leave(index, out_ref.at[:, :, 3 * HALF :])
    for b in range(2):
        for copy in fetches[b]:
            copy.wait()
        for h in range(HEADS):
            lanes = pl.ds(h * HEAD_DIM, HEAD_DIM)
            leave(v.at[b, :, lanes], out_ref.at[h, b, 2 * HALF : 3 * HALF])
        for part, source, scale in (0, q, factor), (1, k, 1.0):
            cos_b, sin_b = cosine[b] * scale, sine[b] * scale
            for h in range(HEADS):
                lanes = slice(h * HEAD_DIM, (h + 1) * HEAD_DIM)
                turned[b, part, h] = turn(source[b, :, lanes], cos_b, sin_b)
            leave(turned.at[b, part], out_ref.at[:, b, part * HALF : (part + 1) * HALF])
    for copy in stores:
        copy.wait()


def pack(starts, queries, keys, values):
    cosine, sine = tables()
    anywhere = pl.BlockSpec(memory_space=pl.ANY)
    rows = pltpu.VMEM((2, HALF, WIDTH), jnp.bfloat16)
    table = pltpu.VMEM((2, HALF, HEAD_DIM), jnp.float32)
    return pl.pallas_call(
        pack_kernel,
        in_specs=[pl.BlockSpec(memory_space=pltpu.SMEM)] + [anywhere] * 5,
        out_specs=anywhere,
        scratch_shapes=[
            rows,
            rows,
            rows,
            table,
            table,
            pltpu.VMEM((2, 2, HEADS, HALF, HEAD_DIM), jnp.bfloat16),
            pltpu.VMEM((HEADS, 2, 16, HEAD_DIM), jnp.bfloat16),
            pltpu.SemaphoreType.DMA((2, 5)),
            pltpu.SemaphoreType.DMA((1 + 2 * (HEADS + 2),)),
        ],
        out_shape=jax.ShapeDtypeStruct((HEADS, 2, ROWS, HEAD_DIM), jnp.bfloat16),
        compiler_params=pltpu.CompilerParams(vmem_limit_bytes=VMEM),
        name="pack",
    )(starts, queries, keys, values, jnp.asarray(cosine), jnp.asarray(sine))


def attention_kernel(packed, o_ref, x_ref, qs, kt, vs, scores, index, pos, got, moved, left, *, tq, width):
    tiles = LEN // tq
    fetches = [
        pltpu.make_async_copy(packed.at[:, :, 3 * HALF :], x_ref.at[:, :, 3 * HALF :], got.at[0]),
        *[
            pltpu.make_async_copy(packed.at[s, :, : 3 * HALF], x_ref.at[s, :, : 3 * HALF], got.at[1 + s])
            for s in range(HEADS)
        ],
    ]
    for fetch in fetches:
        fetch.start()
    vs[:, HEAD_DIM:] = jnp.ones((LEN, HEAD_DIM), jnp.bfloat16)
    fetches[0].wait()
    for t in range(2 * HEADS):
        row = x_ref[t // 2, t % 2, 3 * HALF :, :].astype(jnp.float32)
        index[t : t + 1, :] = row[:1].astype(jnp.int32)
    copy = pltpu.make_async_copy(index, pos, moved)
    copy.start()
    copy.wait()
    for fetch in fetches[1:]:
        fetch.wait()

    def place(t, carry):
        at = pl.ds(pl.multiple_of(pos[t, 0] * HALF, HALF), HALF)
        s, b = t // 2, t % 2
        qs[at, :] = x_ref[s, b, 0:HALF, :]
        kt[:, at] = x_ref[s, b, HALF : 2 * HALF, :].T
        vs[at, :HEAD_DIM] = x_ref[s, b, 2 * HALF : 3 * HALF, :]
        return carry

    lax.fori_loop(0, 2 * HEADS, place, 0, unroll=4)

    row = lax.broadcasted_iota(jnp.int32, (tq, tq), 0)
    col = lax.broadcasted_iota(jnp.int32, (tq, tq), 1)

    def chunks(i):
        seen = (i + 1) * tq
        return [(o, min(width, seen - o)) for o in range(0, seen, width)]

    def score(i, first, count, high):
        s = jnp.dot(
            qs[i * tq : (i + 1) * tq, :],
            kt[:, first : first + count],
            preferred_element_type=jnp.float32,
        )
        if first + count > i * tq:
            before = i * tq - first
            last = jnp.where(col <= row, s[:, before:], -1e30)
            s = jnp.concatenate([s[:, :before], last], axis=1) if before else last
        scores[i % 2, :, first : first + count] = s
        for c in range(0, count, 128):
            part = s[:, c : c + 128]
            high = part if high is None else jnp.maximum(high, part)
        return high

    def weigh(i, first, count, high, total):
        p = jnp.concatenate(
            [
                jnp.exp2(scores[i % 2, :, c : c + 128] - high).astype(jnp.bfloat16)
                for c in range(first, first + count, 128)
            ],
            axis=1,
        )
        part = jnp.dot(p, vs[first : first + count, :], preferred_element_type=jnp.float32)
        return part if total is None else total + part

    high = None
    for chunk in chunks(0):
        high = score(0, *chunk, high)
    for i in range(tiles):
        m = jnp.broadcast_to(jnp.max(high, axis=1, keepdims=True), (tq, 128))
        high = total = None
        mine, following = chunks(i), chunks(i + 1) if i + 1 < tiles else []
        for t in range(max(len(mine), len(following))):
            if t < len(following):
                high = score(i + 1, *following[t], high)
            if t < len(mine):
                total = weigh(i, *mine[t], m, total)
        qs[i * tq : (i + 1) * tq, :] = (total[:, :HEAD_DIM] / total[:, HEAD_DIM:]).astype(
            jnp.bfloat16
        )

    def leave(t):
        from_ = qs.at[pl.ds(pl.multiple_of(pos[t, 0] * HALF, HALF), HALF)]
        return pltpu.make_async_copy(from_, o_ref.at[t // 2, t % 2], left.at[t])

    def start(t, carry):
        leave(t).start()
        return carry

    def wait(t, carry):
        leave(t).wait()
        return carry

    lax.fori_loop(0, 2 * HEADS, start, 0, unroll=8)
    lax.fori_loop(0, 2 * HEADS, wait, 0, unroll=8)


def attention(packed, tq=256, width=1024):
    return pl.pallas_call(
        functools.partial(attention_kernel, tq=tq, width=width),
        out_shape=pltpu.HBM((HEADS, 2, HALF, HEAD_DIM), jnp.bfloat16),
        in_specs=[
            pl.BlockSpec(memory_space=pl.ANY),
        ],
        out_specs=pl.BlockSpec(memory_space=pltpu.HBM),
        scratch_shapes=[
            pltpu.VMEM((HEADS, 2, ROWS, HEAD_DIM), jnp.bfloat16),
            pltpu.VMEM((LEN, HEAD_DIM), jnp.bfloat16),
            pltpu.VMEM((HEAD_DIM, LEN), jnp.bfloat16),
            pltpu.VMEM((LEN, 2 * HEAD_DIM), jnp.bfloat16),
            pltpu.VMEM((2, tq, LEN), jnp.float32),
            pltpu.VMEM((2 * HEADS, 128), jnp.int32),
            pltpu.SMEM((2 * HEADS, 128), jnp.int32),
            pltpu.SemaphoreType.DMA((1 + HEADS,)),
            pltpu.SemaphoreType.DMA,
            pltpu.SemaphoreType.DMA((2 * HEADS,)),
        ],
        compiler_params=pltpu.CompilerParams(vmem_limit_bytes=SMALL),
        cost_estimate=pl.CostEstimate(
            flops=8 * LEN * LEN * HEAD_DIM, bytes_accessed=4 * 2**20, transcendentals=LEN * LEN // 2
        ),
        name="attention",
    )(packed)


PIECES = ((0, 0), (0, 1), (3, 0), (1, 0), (3, 1), (1, 1), (2, 0), (2, 1))
STEP = 512
HALF_D = D // 2
GROUP = WIDTH // 4


def project_kernel(place, att_ref, hidden_ref, own_ref, *refs, half):
    pieces = refs[:7]
    out_ref, heads, left, rows, hidden, acc, out, att_sem, hidden_sem, in_sem, out_sem = refs[-11:]
    core = place[0] if half == 0 else 1 - place[0]
    here = pl.ds(pl.multiple_of(core * HALF_D, HALF_D), HALF_D)
    first, fetches = 0, []
    for n, ref in enumerate([own_ref.at[:, here], *pieces]):
        to = rows.at[first : first + ref.shape[0]]
        fetches.append((first, pltpu.make_async_copy(ref, to, in_sem.at[n])))
        first += ref.shape[0]
    att = pltpu.make_async_copy(att_ref, heads, att_sem)
    residual = pltpu.make_async_copy(hidden_ref.at[:, here], hidden, hidden_sem)
    att.start()
    for _, copy in fetches:
        copy.start()
    residual.start()
    att.wait()
    for n in range(len(PIECES)):
        for i in range(2):
            head = heads[2 * place[1 + n] + i].reshape(2 * HALF, HEAD_DIM)
            left[:, (2 * n + i) * HEAD_DIM : (2 * n + i + 1) * HEAD_DIM] = head
    stores = []
    for group in range(0, WIDTH, GROUP):
        for first, copy in fetches:
            if group <= first < group + GROUP:
                copy.wait()
        if group + GROUP == WIDTH:
            residual.wait()
        for t in range(HALF_D // STEP):
            at = pl.ds(t * STEP, STEP)
            part = jnp.dot(
                left[:, group : group + GROUP],
                rows[group : group + GROUP, at],
                preferred_element_type=jnp.float32,
            )
            if group > 0:
                part += acc[:, at]
            if group + GROUP < WIDTH:
                acc[:, at] = part
            else:
                out[t] = (hidden[:, at].astype(jnp.float32) + part).astype(jnp.bfloat16)
                to = pl.ds(pl.multiple_of(core * HALF_D + t * STEP, STEP), STEP)
                store = pltpu.make_async_copy(out.at[t], out_ref.at[:, to], out_sem.at[t])
                store.start()
                stores.append(store)
    for store in stores:
        store.wait()


def project(half, place, att, hidden, own, pieces, *done):
    hidden = pltpu.with_memory_space_constraint(hidden, pltpu.HBM)
    return pl.pallas_call(
        functools.partial(project_kernel, half=half),
        in_specs=[pl.BlockSpec(memory_space=pltpu.SMEM)]
        + [pl.BlockSpec(memory_space=pl.ANY)] * (10 + len(done)),
        out_specs=pl.BlockSpec(memory_space=pl.ANY),
        scratch_shapes=[
            pltpu.VMEM((HEADS, 2, HALF, HEAD_DIM), jnp.bfloat16),
            pltpu.VMEM((2 * HALF, WIDTH), jnp.bfloat16),
            pltpu.VMEM((WIDTH, HALF_D), jnp.bfloat16),
            pltpu.VMEM((2 * HALF, HALF_D), jnp.bfloat16),
            pltpu.VMEM((2 * HALF, HALF_D), jnp.float32),
            pltpu.VMEM((HALF_D // STEP, 2 * HALF, STEP), jnp.bfloat16),
            pltpu.SemaphoreType.DMA,
            pltpu.SemaphoreType.DMA,
            pltpu.SemaphoreType.DMA((8,)),
            pltpu.SemaphoreType.DMA((HALF_D // STEP,)),
        ],
        out_shape=jax.ShapeDtypeStruct((2 * HALF, D), jnp.bfloat16),
        input_output_aliases={11: 0} if done else {},
        compiler_params=pltpu.CompilerParams(vmem_limit_bytes=SMALL),
        cost_estimate=pl.CostEstimate(
            flops=2 * HALF * WIDTH * D, bytes_accessed=12 * 2**20, transcendentals=0
        ),
        name="project",
    )(place, att, hidden, own, *pieces, *done)


def arrive_kernel(att_ref, out_ref):
    del att_ref, out_ref


def arrive(att):
    return pl.pallas_call(
        arrive_kernel,
        in_specs=[pl.BlockSpec(memory_space=pl.ANY)],
        out_specs=pl.BlockSpec(memory_space=pl.ANY),
        out_shape=jax.ShapeDtypeStruct(att.shape, att.dtype),
        input_output_aliases={0: 0},
        compiler_params=pltpu.CompilerParams(vmem_limit_bytes=SMALL),
        cost_estimate=pl.CostEstimate(
            flops=2 * 10**10, bytes_accessed=2 * 2**20, transcendentals=0
        ),
        name="arrive",
    )(att)


def shards(hidden_in, queries, keys, values, block_start, out_weight):
    y, xh, c = lax.axis_index("y"), lax.axis_index("xh"), lax.axis_index("c")
    packed = pack(block_start, queries[0], keys[0], values[0])
    packed = lax.all_to_all(packed, OWNERS, 0, 0, tiled=True)

    half = lax.dynamic_slice(out_weight, (0, c * (D // 2)), (WIDTH // 8, D // 2))
    mine, other = {}, {}
    mine[0, 1] = send(half, x_over)
    mine[3, 0] = send(half, y_up)
    mine[1, 0] = send(half, y_down)
    second = {
        (3, 1): send(mine[3, 0], x_over),
        (1, 1): send(mine[0, 1], y_down),
        (2, 0): send(mine[3, 0], y_up),
        (2, 1): send(mine[1, 0], x_over_y_down),
    }
    before = mine[3, 0]
    for at in (3, 0), (0, 1):
        piece, _ = lax.optimization_barrier((mine[at], before))
        other[at] = before = send(piece, core_over)

    attended = attention(packed)
    piece, _ = lax.optimization_barrier((mine[1, 0], (attended, before)))
    other[1, 0] = send(piece, core_over)
    second, _ = lax.optimization_barrier((second, other[1, 0]))
    attended = lax.all_to_all(attended, OWNERS, 0, 0, tiled=True)
    for at in second:
        mine[at] = second[at]
        other[at] = send(mine[at], core_over)
    mine = [mine[at] for at in PIECES[1:]]
    other = [other[at] for at in PIECES[1:]]

    owners = [((y + dy) % 4) * 2 + (xh + dx) % 2 for dy, dx in PIECES]
    place = jnp.stack([c, *owners]).astype(jnp.int32)
    attended = arrive(attended)
    done = project(0, place, attended, hidden_in[0], out_weight, mine)
    return project(1, place, attended, hidden_in[0], out_weight, other, done)[None]


def solution(mesh):
    fine = Mesh(mesh.devices.reshape(SIZES), AXES)
    return jax.shard_map(
        shards,
        mesh=fine,
        in_specs=(
            P(FSDP, SEQ, None),
            P(FSDP, SEQ, None),
            P(FSDP, SEQ, None),
            P(FSDP, SEQ, None),
            P(SEQ),
            P(FSDP, None),
        ),
        out_specs=P(FSDP, SEQ, None),
        check_vma=False,
    )
```
